32 devices in a mesh: grp: 2 (over y), ev: 2 (over x), loc: 8 (over z, core).
Axes of the slice: x: 2, y: 2, z: 4, core: 2. Of those that a mesh axis runs over, the one named last changes fastest.
Arguments:
- intensity_bin: int32 [256, 16384], P('ev', ('grp', 'loc')), parts along dimension 1, may hold values from 0 to 62
- bin_fraction: bfloat16 [256, 16384], P('ev', ('grp', 'loc')), parts along dimension 1, may hold values from 0 to 1
- footprint_mask: int32 [256, 128], P('ev', ('grp', 'loc')), parts along dimension 1, may hold values 0 or 1
- location_contract: int32 [16384], P(('grp', 'loc')), parts along dimension 0, may hold values from 0 to 2047
- location_class: int32 [16384], P(('grp', 'loc')), parts along dimension 0, may hold values from 0 to 127
- exposure: float32 [16384], P(('grp', 'loc')), parts along dimension 0, may hold values from 0.32 to 3.2
- curves: float32 [128, 64], replicated, may hold values from 0 to 1
- event_year: int32 [256], P('ev'), may hold values from 0 to 127
- occ_retention: float32 [4096], P('grp'), parts along dimension 0, may hold values from 0.2 to 0.8
- occ_limit: float32 [4096], P('grp'), parts along dimension 0, may hold values from 0.8 to 2.5
- agg_retention: float32 [4096], P('grp'), parts along dimension 0, may hold values from 0.125 to 0.375
- agg_limit: float32 [4096], P('grp'), parts along dimension 0, may hold values from 0.375 to 1
Outputs:
- annual: float32 [4096, 128], P(('grp', 'loc'), 'ev'), parts along dimension 0
- year_mean: float32 [256], P(('grp', 'ev')), parts along dimension 0
The draws below stay inside these ranges and needn't reach their ends.
There are 2 independent parts, one for each index of `grp`. The reference program is written for one: setup_inputs(seed, part) draws one part's arguments, and reference() takes and returns one part's arrays. A program takes and returns all parts, laid end to end along the dimension named above; an argument that names none is the same for every part. Nothing has to cross between parts.
All inputs are finite; a program needn't handle non-finite values. No bound on the sum of `footprint_mask` on one device may be relied on, other than what follows from the above.
Results may differ from the reference program's by a relative error of at most 0.0016.
Values sent between devices are 32-bit elements; how exact they have to be, the bound alone decides.
A program may use at most 64 MiB of HBM per device.

```python
import math
import jax
import jax.numpy as jnp
from jax import lax

CONTRACTS = 2048
KNOTS = 64
CURVES = 128
BLOCK = 128
EVENTS = 256
LOCATIONS = 8192
YEARS = 128


def plant(result, own_key, least, top_value):
    place = [jax.random.randint(jax.random.fold_in(own_key, axis), (), 0, length) for axis, length in enumerate(result.shape)]
    widest = result.shape.index(max(result.shape))
    next_to = place[:widest] + [(place[widest] + 1) % result.shape[widest]] + place[widest + 1:]
    return result.at[tuple(place)].set(least).at[tuple(next_to)].set(top_value)


def block_levels(key, shape, cuts, least, largest):
    def one(position, parts):
        steps = jax.random.uniform(jax.random.fold_in(jax.random.fold_in(key, 6), position), (parts,), jnp.float32, least / len(cuts), largest / len(cuts))
        return jnp.repeat(jnp.exp(steps), shape[position] // parts).reshape((-1,) + (1,) * (len(shape) - position - 1))

    factor_of = one(*cuts[0])
    for cut in cuts[1:]:
        factor_of = factor_of * one(*cut)
    return factor_of


def setup_inputs(seed: int = 0, part: int = 0) -> dict:
    key_list = jax.random.split(jax.random.key(seed), 13)
    own_keys = jax.random.split(jax.random.fold_in(key_list[12], part), 13)
    return {
        "intensity_bin": plant(jax.random.randint(own_keys[0], (EVENTS, LOCATIONS), 0, KNOTS - 1), jax.random.fold_in(own_keys[0], 1), 0, (KNOTS - 1) - 1).astype(jnp.int32),
        "bin_fraction": jnp.clip(1.0 * jax.random.uniform(own_keys[1], (EVENTS, LOCATIONS), jnp.float32) ** block_levels(own_keys[1], (EVENTS, LOCATIONS), ((0, 2), (1, 8)), -0.2, 0.2), 0.0, 1.0).astype(jnp.bfloat16),
        "footprint_mask": plant((jax.random.randint(own_keys[2], (EVENTS, LOCATIONS // BLOCK), 0, 2) < 1).astype(jnp.int32), jax.random.fold_in(own_keys[2], 1), 0, 1),
        "location_contract": plant(jax.random.randint(own_keys[3], (LOCATIONS,), 0, CONTRACTS), jax.random.fold_in(own_keys[3], 1), 0, CONTRACTS - 1).astype(jnp.int32),
        "location_class": plant(jax.random.randint(own_keys[4], (LOCATIONS,), 0, CURVES), jax.random.fold_in(own_keys[4], 1), 0, CURVES - 1).astype(jnp.int32),
        "exposure": jnp.clip(jnp.exp(math.log(3.2) - 2.3025851 * jax.random.uniform(own_keys[5], (LOCATIONS,), jnp.float32) ** block_levels(own_keys[5], (LOCATIONS,), ((0, 8),), -0.2, 0.2)), 0.32, 3.2),
        "curves": jnp.clip(jax.random.uniform(key_list[6], (CURVES, KNOTS), jnp.float32, 0.0, 1.0), 0.0, 1.0),
        "event_year": plant(jax.random.randint(key_list[7], (EVENTS,), 0, YEARS), jax.random.fold_in(key_list[7], 1), 0, YEARS - 1).astype(jnp.int32),
        "occ_retention": jnp.clip(jax.random.uniform(own_keys[8], (CONTRACTS,), jnp.float32, 0.2, 0.8), 0.2, 0.8),
        "occ_limit": jnp.clip(jax.random.uniform(own_keys[9], (CONTRACTS,), jnp.float32, 0.8, 2.5), 0.8, 2.5),
        "agg_retention": jnp.clip(jax.random.uniform(own_keys[10], (CONTRACTS,), jnp.float32, 0.125, 0.375), 0.125, 0.375),
        "agg_limit": jnp.clip(jax.random.uniform(own_keys[11], (CONTRACTS,), jnp.float32, 0.375, 1.0), 0.375, 1.0),
    }


def reference(intensity_bin, bin_fraction, footprint_mask, location_contract, location_class, exposure, curves, event_year, occ_retention, occ_limit, agg_retention, agg_limit):
    curve_rows = curves[location_class]
    width = math.gcd(EVENTS, 64)
    count = EVENTS // width
    bins_all = intensity_bin.reshape(count, width, LOCATIONS)
    frac_all = bin_fraction.reshape(count, width, LOCATIONS)
    mask_all = footprint_mask.reshape(count, width, LOCATIONS // BLOCK)
    places = jnp.arange(LOCATIONS, dtype=jnp.int32)[None, :]

    def one_block(pieces):
        bins, frac, mask = pieces
        low = curve_rows[places, bins]
        high = curve_rows[places, bins + 1]
        fval = frac.astype(jnp.float32)
        damage = (1.0 - fval) * low + fval * high
        keep = jnp.repeat(mask.astype(jnp.float32), BLOCK, axis=1)
        loss = (damage * keep * exposure[None, :]).astype(jnp.bfloat16)
        return jax.ops.segment_sum(loss.astype(jnp.float32).T, location_contract, num_segments=CONTRACTS)

    blocks = lax.map(one_block, (bins_all, frac_all, mask_all))
    totals = jnp.transpose(blocks, (1, 0, 2)).reshape(CONTRACTS, EVENTS)
    occurrence = jnp.minimum(jnp.maximum(totals - occ_retention[:, None], 0.0), occ_limit[:, None])
    year_onehot = (event_year[:, None] == jnp.arange(YEARS, dtype=jnp.int32)[None, :]).astype(jnp.float32)
    yearly = jnp.dot(occurrence, year_onehot, precision=lax.Precision.HIGHEST, preferred_element_type=jnp.float32)
    annual = jnp.minimum(jnp.maximum(yearly - agg_retention[:, None], 0.0), agg_limit[:, None])
    year_mean = jnp.sum(annual, axis=0) / CONTRACTS
    return annual, year_mean
```

```python
import functools

import jax
import jax.numpy as jnp
from jax import lax
from jax.experimental import pallas as pl
from jax.experimental.pallas import tpu as pltpu
from jax.sharding import PartitionSpec as P

YR_DEV = 64
CORES = 2
LANES = 128
MESH = pl.DeviceIdType.MESH
F32, BF16, I32 = jnp.float32, jnp.bfloat16, jnp.int32

NT = (((1,), (1,)), ((), ()))
TN = (((0,), (0,)), ((), ()))


def iota(shape, axis):
    return lax.broadcasted_iota(I32, shape, axis)


def split(x):
    high = x.astype(BF16)
    return high, (x - high.astype(F32)).astype(BF16)


def kernel(
    n_loc,
    n_ev,
    bins_ref,
    frac_ref,
    mask_ref,
    contract_ref,
    class_ref,
    expo_ref,
    curves_ref,
    year_ref,
    oret_ref,
    olim_ref,
    aret_ref,
    alim_ref,
    annual_ref,
    mean_ref,
    spread,
    psib,
    own,
    sibr,
    upr,
    dnr,
    ybuf,
    yrecv,
    msend,
    mrecv,
    sib_send,
    sib_recv,
    up_send,
    up_recv,
    dn_send,
    dn_recv,
    y_send,
    y_recv,
    m_send,
    m_recv,
):
    nz = n_loc // CORES
    events, locs = bins_ref.shape
    blocks = mask_ref.shape[1]
    wide = locs // blocks
    curve_count, knots = curves_ref.shape
    share = annual_ref.shape[0]
    chip = share * CORES
    contracts = share * n_loc
    chunk = ybuf.shape[3]
    chunks = share // chunk

    me = lax.axis_index("loc")
    ev = lax.axis_index("ev")
    z, core = me // CORES, me % CORES
    other = 1 - core
    sibling = z * CORES + other

    barrier = pltpu.get_barrier_semaphore()
    for k in range(1, n_loc):
        pl.semaphore_signal(
            barrier, inc=1, device_id={"loc": lax.rem(me + k, n_loc)}, device_id_type=MESH
        )
    for k in range(1, n_ev):
        pl.semaphore_signal(
            barrier, inc=1, device_id={"ev": lax.rem(ev + k, n_ev)}, device_id_type=MESH
        )

    curves = curves_ref[...]
    steps = jnp.concatenate(
        [curves[:, 1:] - curves[:, :-1], jnp.zeros((curve_count, 1), F32)], axis=1
    )
    c_high, c_low = split(jnp.concatenate([curves, steps], axis=1))
    blank = jnp.zeros((curve_count, LANES), BF16)
    first_row = (iota((16, LANES), 0) == 0).astype(F32).astype(BF16)
    table_rhs = jnp.concatenate(
        [
            jnp.concatenate([c_high, c_high, c_low, jnp.zeros((16, LANES), BF16)], axis=0),
            jnp.concatenate([blank, blank, blank, first_row], axis=0),
        ],
        axis=1,
    )
    eye = (iota((blocks, blocks), 0) == iota((blocks, blocks), 1)).astype(F32).astype(BF16)
    keep = lax.dot_general(
        eye, mask_ref[...].astype(F32).astype(BF16), NT, preferred_element_type=F32
    )
    rows_in_chip = []
    for b in range(blocks):
        cols = pl.ds(b * wide, wide)
        contract = contract_ref[b : b + 1, :]
        where_chip = jnp.zeros_like(contract)
        for t in range(1, nz):
            where_chip += (contract >= t * chip).astype(I32)
        rows_in_chip.append(contract - where_chip * chip)
        weight = jnp.where(
            iota((curve_count, wide), 0) == class_ref[b : b + 1, :], expo_ref[b : b + 1, :], 0.0
        )
        w_high, w_low = split(weight)
        chip_rows = jnp.where(iota((16, wide), 0) == 0, where_chip.astype(F32), 0.0).astype(BF16)
        lhs = jnp.concatenate([w_high, w_low, w_high, chip_rows], axis=0)
        both = lax.dot_general(lhs, table_rhs, TN, preferred_element_type=F32)
        table, home = both[:, :LANES], both[:, LANES:]
        place = (bins_ref[:, cols].astype(F32) + frac_ref[:, cols].astype(F32)).T
        knot = place.astype(I32)
        part = place - knot.astype(F32)
        low = jnp.take_along_axis(table, knot, axis=1, mode="promise_in_bounds")
        rise = jnp.take_along_axis(table, knot + knots, axis=1, mode="promise_in_bounds")
        loss = (low + part * rise) * keep[b : b + 1, :]
        for t in range(nz):
            spread[cols, pl.ds(t * events, events)] = jnp.where(home == t, loss, 0.0).astype(BF16)

    def partial(which):
        member = jnp.concatenate(
            [
                (iota((share, wide), 0) + which * share == rows).astype(F32).astype(BF16)
                for rows in rows_in_chip
            ],
            axis=1,
        )
        return jnp.dot(member, spread[...], preferred_element_type=F32)

    sums = partial(other)
    for t in range(nz):
        psib[t] = sums[:, t * events : (t + 1) * events]

    pl.semaphore_wait(barrier, n_loc - 1 + n_ev - 1)

    def sib_copy(t):
        return pltpu.make_async_remote_copy(
            src_ref=psib.at[t],
            dst_ref=sibr.at[t],
            send_sem=sib_send.at[t],
            recv_sem=sib_recv.at[t],
            device_id={"loc": sibling},
            device_id_type=MESH,
        )

    order = []
    for t in range((nz + 1) // 2):
        order += [t] if t == nz - 1 - t else [nz - 1 - t, t]
    for t in order:
        sib_copy(t).start()

    sums = partial(core)
    for t in range(nz):
        own[t] = sums[:, t * events : (t + 1) * events]

    first = me * share

    def row_of(ref, c):
        start = first + c * chunk
        row = ref[pl.ds(start // LANES, 1), :]
        if share % LANES:
            row = pltpu.roll(
                jnp.broadcast_to(row, (8, LANES)), (LANES - start % LANES) % LANES, 1
            )[:1]
        return row[:, :chunk]

    def column_of(ref, c):
        row = jnp.broadcast_to(row_of(ref, c), (chunk, chunk))
        return jnp.sum(
            jnp.where(iota((chunk, chunk), 0) == iota((chunk, chunk), 1), row, 0.0),
            axis=1,
            keepdims=True,
        )

    orets = [column_of(oret_ref, c) for c in range(chunks)]
    olims = [column_of(olim_ref, c) for c in range(chunks)]
    year_rows = (iota((n_ev * YR_DEV, events), 0) == year_ref[...]).astype(F32).astype(BF16)
    year_rows = jnp.concatenate([year_rows, year_rows], axis=1)

    def hop(t, c, send, recv, into, step):
        rows = pl.ds(c * chunk, chunk)
        return pltpu.make_async_remote_copy(
            src_ref=own.at[t, rows],
            dst_ref=into.at[t, rows],
            send_sem=send.at[t, c],
            recv_sem=recv.at[t, c],
            device_id={"loc": me + step},
            device_id_type=MESH,
        )

    up = functools.partial(hop, send=up_send, recv=up_recv, into=upr, step=CORES)
    down = functools.partial(hop, send=dn_send, recv=dn_recv, into=dnr, step=-CORES)

    def pass_on(t, c, way, into, inner):
        rows = pl.ds(c * chunk, chunk)
        if c == 0:
            sib_copy(t).wait_recv()

        @pl.when(inner)
        def _():
            way(t, c).wait_recv()
            own[t, rows] = own[t, rows] + sibr[t, rows] + into[t, rows]

        @pl.when(jnp.logical_not(inner))
        def _():
            own[t, rows] = own[t, rows] + sibr[t, rows]

        way(t, c).start()

    for tau in range(nz - 1):
        for c in range(chunks):

            @pl.when(z <= tau)
            def _():
                pass_on(nz - 1 - tau + z, c, up, upr, z > 0)

            @pl.when(nz - 1 - z <= tau)
            def _():
                pass_on(tau - (nz - 1) + z, c, down, dnr, z < nz - 1)

    def year_copy(c, k):
        return pltpu.make_async_remote_copy(
            src_ref=ybuf.at[c, lax.rem(ev + k, n_ev)],
            dst_ref=yrecv.at[c, k - 1],
            send_sem=y_send.at[c, k - 1],
            recv_sem=y_recv.at[c, k - 1],
            device_id={"ev": lax.rem(ev + k, n_ev)},
            device_id_type=MESH,
        )

    sib_copy(z).wait_recv()
    for c in range(chunks):
        rows = pl.ds(c * chunk, chunk)
        own[z, rows] = own[z, rows] + sibr[z, rows]

        @pl.when(z > 0)
        def _():
            up(z, c).wait_recv()
            own[z, rows] = own[z, rows] + upr[z, rows]

        @pl.when(z < nz - 1)
        def _():
            down(z, c).wait_recv()
            own[z, rows] = own[z, rows] + dnr[z, rows]

        occurrence = jnp.minimum(jnp.maximum(own[z, rows] - orets[c], 0.0), olims[c])
        years = lax.dot_general(
            year_rows,
            jnp.concatenate(split(occurrence), axis=1),
            NT,
            preferred_element_type=F32,
        )
        for j in range(n_ev):
            ybuf[c, j] = years[j * YR_DEV : (j + 1) * YR_DEV]
        for k in range(1, n_ev):
            year_copy(c, k).start()

    total = jnp.zeros((1, YR_DEV), F32)
    for c in range(chunks):
        yearly = ybuf[c, ev]
        for k in range(1, n_ev):
            year_copy(c, k).wait_recv()
            yearly += yrecv[c, k - 1]
        annual = jnp.minimum(
            jnp.maximum(yearly - row_of(aret_ref, c), 0.0), row_of(alim_ref, c)
        )
        annual = annual.T
        annual_ref[c * chunk : (c + 1) * chunk, :] = annual
        total += jnp.sum(annual, axis=0, keepdims=True)

    msend[:, :YR_DEV] = jnp.broadcast_to(total, (8, YR_DEV))
    msend[:, YR_DEV:] = jnp.zeros((8, LANES - YR_DEV), F32)

    def mean_copy(k):
        return pltpu.make_async_remote_copy(
            src_ref=msend,
            dst_ref=mrecv.at[k - 1],
            send_sem=m_send.at[k - 1],
            recv_sem=m_recv.at[k - 1],
            device_id={"loc": lax.rem(me + k, n_loc)},
            device_id_type=MESH,
        )

    for k in range(1, n_loc):
        mean_copy(k).start()

    for t in range(nz):
        sib_copy(t).wait_send()
    for tau in range(nz - 1):
        for c in range(chunks):

            @pl.when(z <= tau)
            def _():
                up(nz - 1 - tau + z, c).wait_send()

            @pl.when(nz - 1 - z <= tau)
            def _():
                down(tau - (nz - 1) + z, c).wait_send()

    for c in range(chunks):
        for k in range(1, n_ev):
            year_copy(c, k).wait_send()

    mean = msend[...]
    for k in range(1, n_loc):
        mean_copy(k).wait_recv()
        mean += mrecv[k - 1]
    mean_ref[...] = (mean / contracts)[:1, :YR_DEV]
    for k in range(1, n_loc):
        mean_copy(k).wait_send()


def solution(mesh):
    n_loc, n_ev = mesh.shape["loc"], mesh.shape["ev"]
    nz = n_loc // CORES

    def local(bins, frac, mask, contract, which, expo, curves, year, oret, olim, aret, alim):
        events, locs = bins.shape
        share = oret.shape[0] // n_loc
        chunk = min(share, LANES)
        chunks = share // chunk
        dma = pltpu.SemaphoreType.DMA
        pieces = pltpu.VMEM((nz, share, events), F32)
        lanes = lambda x: x.reshape(-1, LANES)
        annual, mean = pl.pallas_call(
            functools.partial(kernel, n_loc, n_ev),
            out_shape=(
                jax.ShapeDtypeStruct((share, YR_DEV), F32),
                jax.ShapeDtypeStruct((1, YR_DEV), F32),
            ),
            in_specs=[pl.BlockSpec(memory_space=pltpu.VMEM)] * 12,
            out_specs=(pl.BlockSpec(memory_space=pltpu.VMEM),) * 2,
            scratch_shapes=[
                pltpu.VMEM((locs, nz * events), BF16),
                pieces,
                pieces,
                pieces,
                pieces,
                pieces,
                pltpu.VMEM((chunks, n_ev, YR_DEV, chunk), F32),
                pltpu.VMEM((chunks, n_ev - 1, YR_DEV, chunk), F32),
                pltpu.VMEM((8, LANES), F32),
                pltpu.VMEM((n_loc - 1, 8, LANES), F32),
                dma((nz,)),
                dma((nz,)),
                dma((nz, chunks)),
                dma((nz, chunks)),
                dma((nz, chunks)),
                dma((nz, chunks)),
                dma((chunks, n_ev - 1)),
                dma((chunks, n_ev - 1)),
                dma((n_loc - 1,)),
                dma((n_loc - 1,)),
            ],
            compiler_params=pltpu.CompilerParams(
                collective_id=0, has_side_effects=True, vmem_limit_bytes=48 * 2**20
            ),
        )(
            bins,
            frac,
            mask,
            lanes(contract),
            lanes(which),
            lanes(expo),
            curves,
            lanes(year),
            lanes(oret),
            lanes(olim),
            lanes(aret),
            lanes(alim),
        )
        return annual, mean.reshape(YR_DEV)

    part = ("grp", "loc")
    in_specs = (
        P("ev", part),
        P("ev", part),
        P("ev", part),
        P(part),
        P(part),
        P(part),
        P(),
        P("ev"),
        P("grp"),
        P("grp"),
        P("grp"),
        P("grp"),
    )
    out_specs = (P(part, "ev"), P(("grp", "ev")))
    return jax.shard_map(local, mesh=mesh, in_specs=in_specs, out_specs=out_specs, check_vma=False)
```

```python
import functools
import math

import jax
import jax.numpy as jnp
from jax import lax
from jax.experimental import pallas as pl
from jax.experimental.pallas import tpu as pltpu
from jax.sharding import PartitionSpec as P

YR_DEV = 64
CORES = 2
LANES = 128
MESH = pl.DeviceIdType.MESH
F32, BF16, I32 = jnp.float32, jnp.bfloat16, jnp.int32

NT = (((1,), (1,)), ((), ()))
TN = (((0,), (0,)), ((), ()))


def iota(shape, axis):
    return lax.broadcasted_iota(I32, shape, axis)


def split(x):
    high = x.astype(BF16)
    return high, (x - high.astype(F32)).astype(BF16)


def kernel(
    n_loc,
    n_ev,
    bins_hbm,
    frac_hbm,
    mask_hbm,
    contract_hbm,
    class_hbm,
    expo_hbm,
    curves_hbm,
    year_hbm,
    oret_hbm,
    olim_hbm,
    aret_hbm,
    alim_hbm,
    annual_ref,
    mean_ref,
    bins_ref,
    frac_ref,
    mask_ref,
    contract_ref,
    class_ref,
    expo_ref,
    curves_ref,
    year_ref,
    oret_ref,
    olim_ref,
    aret_ref,
    alim_ref,
    wide_sem,
    small_sem,
    spread,
    psib,
    own,
    sibr,
    upr,
    dnr,
    ybuf,
    yrecv,
    msend,
    mrecv,
    sib_send,
    sib_recv,
    up_send,
    up_recv,
    dn_send,
    dn_recv,
    y_send,
    y_recv,
    m_send,
    m_recv,
):
    nz = n_loc // CORES
    events, locs = bins_ref.shape
    blocks = mask_ref.shape[0]
    wide = locs // blocks
    knots, curve_count = curves_ref.shape
    share = annual_ref.shape[1]
    chip = share * CORES
    contracts = share * n_loc
    chunk = ybuf.shape[3]
    chunks = share // chunk

    me = lax.axis_index("loc")
    ev = lax.axis_index("ev")
    z, core = me // CORES, me % CORES
    other = 1 - core
    sibling = z * CORES + other

    small = [
        pltpu.make_async_copy(source, target, small_sem.at[i])
        for i, (source, target) in enumerate(
            (
                (curves_hbm, curves_ref),
                (class_hbm, class_ref),
                (expo_hbm, expo_ref),
                (contract_hbm, contract_ref),
                (mask_hbm, mask_ref),
                (year_hbm, year_ref),
                (oret_hbm, oret_ref),
                (olim_hbm, olim_ref),
                (aret_hbm, aret_ref),
                (alim_hbm, alim_ref),
            )
        )
    ]
    loads = wide_sem.shape[1]
    load_cols = locs // loads
    wides = [
        [
            pltpu.make_async_copy(
                source.at[:, pl.ds(i * load_cols, load_cols)],
                target.at[:, pl.ds(i * load_cols, load_cols)],
                wide_sem.at[j, i],
            )
            for j, (source, target) in enumerate(((bins_hbm, bins_ref), (frac_hbm, frac_ref)))
        ]
        for i in range(loads)
    ]
    for copy in small[:5] + [copy for pair in wides for copy in pair] + small[5:]:
        copy.start()

    barrier = pltpu.get_barrier_semaphore()
    for k in range(1, n_loc):
        pl.semaphore_signal(
            barrier, inc=1, device_id={"loc": lax.rem(me + k, n_loc)}, device_id_type=MESH
        )
    for k in range(1, n_ev):
        pl.semaphore_signal(
            barrier, inc=1, device_id={"ev": lax.rem(ev + k, n_ev)}, device_id_type=MESH
        )

    for copy in small[:5]:
        copy.wait()
    curves = curves_ref[...]
    steps = jnp.concatenate([curves[1:] - curves[:-1], jnp.zeros((1, curve_count), F32)], axis=0)
    c_high, c_low = split(jnp.concatenate([curves, steps], axis=0).T)
    blank = jnp.zeros((curve_count, LANES), BF16)
    first_row = (iota((16, LANES), 0) == 0).astype(F32).astype(BF16)
    table_rhs = jnp.concatenate(
        [
            jnp.concatenate([c_high, c_high, c_low, jnp.zeros((16, LANES), BF16)], axis=0),
            jnp.concatenate([blank, blank, blank, first_row], axis=0),
        ],
        axis=1,
    )
    keep = mask_ref[...].astype(F32)
    rows_in_chip = []
    for b in range(blocks):
        cols = pl.ds(b * wide, wide)
        if b * wide % load_cols == 0:
            for copy in wides[b * wide // load_cols]:
                copy.wait()
        contract = contract_ref[b : b + 1, :]
        where_chip = jnp.zeros_like(contract)
        for t in range(1, nz):
            where_chip += (contract >= t * chip).astype(I32)
        rows_in_chip.append(contract - where_chip * chip)
        weight = jnp.where(
            iota((curve_count, wide), 0) == class_ref[b : b + 1, :], expo_ref[b : b + 1, :], 0.0
        )
        w_high, w_low = split(weight)
        chip_rows = jnp.where(iota((16, wide), 0) == 0, where_chip.astype(F32), 0.0).astype(BF16)
        lhs = jnp.concatenate([w_high, w_low, w_high, chip_rows], axis=0)
        both = lax.dot_general(lhs, table_rhs, TN, preferred_element_type=F32)
        table, home = both[:, :LANES], both[:, LANES:]
        place = (bins_ref[:, cols].astype(F32) + frac_ref[:, cols].astype(F32)).T
        knot = place.astype(I32)
        part = place - knot.astype(F32)
        low = jnp.take_along_axis(table, knot, axis=1, mode="promise_in_bounds")
        rise = jnp.take_along_axis(table, knot + knots, axis=1, mode="promise_in_bounds")
        loss = (low + part * rise) * keep[b : b + 1, :]
        for t in range(nz):
            spread[cols, pl.ds(t * events, events)] = jnp.where(home == t, loss, 0.0).astype(BF16)

    def partial(which):
        member = jnp.concatenate(
            [
                (iota((share, wide), 0) + which * share == rows).astype(F32).astype(BF16)
                for rows in rows_in_chip
            ],
            axis=1,
        )
        return jnp.dot(member, spread[...], preferred_element_type=F32)

    sums = partial(other)
    for t in range(nz):
        psib[t] = sums[:, t * events : (t + 1) * events]

    pl.semaphore_wait(barrier, n_loc - 1 + n_ev - 1)

    def sib_copy(t):
        return pltpu.make_async_remote_copy(
            src_ref=psib.at[t],
            dst_ref=sibr.at[t],
            send_sem=sib_send.at[t],
            recv_sem=sib_recv.at[t],
            device_id={"loc": sibling},
            device_id_type=MESH,
        )

    order = []
    for t in range((nz + 1) // 2):
        order += [t] if t == nz - 1 - t else [nz - 1 - t, t]
    for t in order:
        sib_copy(t).start()

    sums = partial(core)
    for t in range(nz):
        own[t] = sums[:, t * events : (t + 1) * events]

    for copy in small[5:]:
        copy.wait()
    first = me * share

    def row_of(ref, c):
        start = first + c * chunk
        row = ref[pl.ds(start // LANES, 1), :]
        if share % LANES:
            row = pltpu.roll(
                jnp.broadcast_to(row, (8, LANES)), (LANES - start % LANES) % LANES, 1
            )[:1]
        return row[:, :chunk]

    def column_of(ref, c):
        row = jnp.broadcast_to(row_of(ref, c), (chunk, chunk))
        return jnp.sum(
            jnp.where(iota((chunk, chunk), 0) == iota((chunk, chunk), 1), row, 0.0),
            axis=1,
            keepdims=True,
        )

    orets = [column_of(oret_ref, c) for c in range(chunks)]
    olims = [column_of(olim_ref, c) for c in range(chunks)]
    year_rows = (iota((n_ev * YR_DEV, events), 0) == year_ref[...]).astype(F32).astype(BF16)
    year_rows = jnp.concatenate([year_rows, year_rows], axis=1)

    def hop(t, c, send, recv, into, step):
        rows = pl.ds(c * chunk, chunk)
        return pltpu.make_async_remote_copy(
            src_ref=own.at[t, rows],
            dst_ref=into.at[t, rows],
            send_sem=send.at[t, c],
            recv_sem=recv.at[t, c],
            device_id={"loc": me + step},
            device_id_type=MESH,
        )

    up = functools.partial(hop, send=up_send, recv=up_recv, into=upr, step=CORES)
    down = functools.partial(hop, send=dn_send, recv=dn_recv, into=dnr, step=-CORES)

    def pass_on(t, c, way, into, inner):
        rows = pl.ds(c * chunk, chunk)
        if c == 0:
            sib_copy(t).wait_recv()

        @pl.when(inner)
        def _():
            way(t, c).wait_recv()
            own[t, rows] = own[t, rows] + sibr[t, rows] + into[t, rows]

        @pl.when(jnp.logical_not(inner))
        def _():
            own[t, rows] = own[t, rows] + sibr[t, rows]

        way(t, c).start()

    for tau in range(nz - 1):
        for c in range(chunks):

            @pl.when(z <= tau)
            def _():
                pass_on(nz - 1 - tau + z, c, up, upr, z > 0)

            @pl.when(nz - 1 - z <= tau)
            def _():
                pass_on(tau - (nz - 1) + z, c, down, dnr, z < nz - 1)

    def year_copy(c, k):
        return pltpu.make_async_remote_copy(
            src_ref=ybuf.at[c, lax.rem(ev + k, n_ev)],
            dst_ref=yrecv.at[c, k - 1],
            send_sem=y_send.at[c, k - 1],
            recv_sem=y_recv.at[c, k - 1],
            device_id={"ev": lax.rem(ev + k, n_ev)},
            device_id_type=MESH,
        )

    sib_copy(z).wait_recv()
    for c in range(chunks):
        rows = pl.ds(c * chunk, chunk)
        own[z, rows] = own[z, rows] + sibr[z, rows]

        @pl.when(z > 0)
        def _():
            up(z, c).wait_recv()
            own[z, rows] = own[z, rows] + upr[z, rows]

        @pl.when(z < nz - 1)
        def _():
            down(z, c).wait_recv()
            own[z, rows] = own[z, rows] + dnr[z, rows]

        occurrence = jnp.minimum(jnp.maximum(own[z, rows] - orets[c], 0.0), olims[c])
        years = lax.dot_general(
            year_rows,
            jnp.concatenate(split(occurrence), axis=1),
            NT,
            preferred_element_type=F32,
        )
        for j in range(n_ev):
            ybuf[c, j] = years[j * YR_DEV : (j + 1) * YR_DEV]
        for k in range(1, n_ev):
            year_copy(c, k).start()

    total = jnp.zeros((1, YR_DEV), F32)
    for c in range(chunks):
        yearly = ybuf[c, ev]
        for k in range(1, n_ev):
            year_copy(c, k).wait_recv()
            yearly += yrecv[c, k - 1]
        annual = jnp.minimum(
            jnp.maximum(yearly - row_of(aret_ref, c), 0.0), row_of(alim_ref, c)
        )
        annual_ref[:, c * chunk : (c + 1) * chunk] = annual
        total += jnp.sum(annual.T, axis=0, keepdims=True)

    msend[:, :YR_DEV] = jnp.broadcast_to(total, (8, YR_DEV))
    msend[:, YR_DEV:] = jnp.zeros((8, LANES - YR_DEV), F32)

    def mean_copy(k):
        return pltpu.make_async_remote_copy(
            src_ref=msend,
            dst_ref=mrecv.at[k - 1],
            send_sem=m_send.at[k - 1],
            recv_sem=m_recv.at[k - 1],
            device_id={"loc": lax.rem(me + k, n_loc)},
            device_id_type=MESH,
        )

    for k in range(1, n_loc):
        mean_copy(k).start()

    for t in range(nz):
        sib_copy(t).wait_send()
    for tau in range(nz - 1):
        for c in range(chunks):

            @pl.when(z <= tau)
            def _():
                up(nz - 1 - tau + z, c).wait_send()

            @pl.when(nz - 1 - z <= tau)
            def _():
                down(tau - (nz - 1) + z, c).wait_send()

    for c in range(chunks):
        for k in range(1, n_ev):
            year_copy(c, k).wait_send()

    mean = msend[...]
    for k in range(1, n_loc):
        mean_copy(k).wait_recv()
        mean += mrecv[k - 1]
    mean_ref[...] = (mean / contracts)[:1, :YR_DEV]
    for k in range(1, n_loc):
        mean_copy(k).wait_send()


def solution(mesh):
    n_loc, n_ev = mesh.shape["loc"], mesh.shape["ev"]
    nz = n_loc // CORES

    def local(bins, frac, mask, contract, which, expo, curves, year, oret, olim, aret, alim):
        events, locs = bins.shape
        share = oret.shape[0] // n_loc
        chunk = min(share, LANES)
        chunks = share // chunk
        dma = pltpu.SemaphoreType.DMA
        pieces = pltpu.VMEM((nz, share, events), F32)
        lanes = lambda x: x.reshape(-1, LANES)
        arguments = (
            bins,
            frac,
            mask.T,
            lanes(contract),
            lanes(which),
            lanes(expo),
            curves.T,
            lanes(year),
            lanes(oret),
            lanes(olim),
            lanes(aret),
            lanes(alim),
        )
        annual, mean = pl.pallas_call(
            functools.partial(kernel, n_loc, n_ev),
            out_shape=(
                jax.ShapeDtypeStruct((YR_DEV, share), F32),
                jax.ShapeDtypeStruct((1, YR_DEV), F32),
            ),
            in_specs=[pl.BlockSpec(memory_space=pltpu.HBM)] * 12,
            out_specs=(pl.BlockSpec(memory_space=pltpu.VMEM),) * 2,
            scratch_shapes=[pltpu.VMEM(x.shape, x.dtype) for x in arguments]
            + [
                dma((2, math.gcd(mask.shape[1], 4))),
                dma((10,)),
                pltpu.VMEM((locs, nz * events), BF16),
                pieces,
                pieces,
                pieces,
                pieces,
                pieces,
                pltpu.VMEM((chunks, n_ev, YR_DEV, chunk), F32),
                pltpu.VMEM((chunks, n_ev - 1, YR_DEV, chunk), F32),
                pltpu.VMEM((8, LANES), F32),
                pltpu.VMEM((n_loc - 1, 8, LANES), F32),
                dma((nz,)),
                dma((nz,)),
                dma((nz, chunks)),
                dma((nz, chunks)),
                dma((nz, chunks)),
                dma((nz, chunks)),
                dma((chunks, n_ev - 1)),
                dma((chunks, n_ev - 1)),
                dma((n_loc - 1,)),
                dma((n_loc - 1,)),
            ],
            compiler_params=pltpu.CompilerParams(
                collective_id=0, has_side_effects=True, vmem_limit_bytes=60 * 2**20
            ),
        )(*arguments)
        return annual.T, mean.reshape(YR_DEV)

    part = ("grp", "loc")
    in_specs = (
        P("ev", part),
        P("ev", part),
        P("ev", part),
        P(part),
        P(part),
        P(part),
        P(),
        P("ev"),
        P("grp"),
        P("grp"),
        P("grp"),
        P("grp"),
    )
    out_specs = (P(part, "ev"), P(("grp", "ev")))
    return jax.shard_map(local, mesh=mesh, in_specs=in_specs, out_specs=out_specs, check_vma=False)
```

```python
import functools
import math

import jax
import jax.numpy as jnp
from jax import lax
from jax.experimental import pallas as pl
from jax.experimental.pallas import tpu as pltpu
from jax.sharding import PartitionSpec as P

YR_DEV = 64
CORES = 2
LANES = 128
MESH = pl.DeviceIdType.MESH
F32, BF16, I32 = jnp.float32, jnp.bfloat16, jnp.int32

NT = (((1,), (1,)), ((), ()))
TN = (((0,), (0,)), ((), ()))


def iota(shape, axis):
    return lax.broadcasted_iota(I32, shape, axis)


def split(x):
    high = x.astype(BF16)
    return high, (x - high.astype(F32)).astype(BF16)


def kernel(
    n_loc,
    n_ev,
    bins_hbm,
    frac_hbm,
    mask_hbm,
    contract_hbm,
    class_hbm,
    expo_hbm,
    curves_hbm,
    year_hbm,
    oret_hbm,
    olim_hbm,
    aret_hbm,
    alim_hbm,
    annual_ref,
    mean_ref,
    bins_ref,
    frac_ref,
    mask_ref,
    contract_ref,
    class_ref,
    expo_ref,
    curves_ref,
    year_ref,
    oret_ref,
    olim_ref,
    aret_ref,
    alim_ref,
    wide_sem,
    small_sem,
    spread,
    psib,
    own,
    sibr,
    upr,
    dnr,
    ybuf,
    yrecv,
    msend,
    mrecv,
    sib_send,
    sib_recv,
    up_send,
    up_recv,
    dn_send,
    dn_recv,
    y_send,
    y_recv,
    m_send,
    m_recv,
):
    nz = n_loc // CORES
    events, locs = bins_ref.shape
    blocks = mask_ref.shape[0]
    wide = locs // blocks
    knots, curve_count = curves_ref.shape
    share = annual_ref.shape[1]
    chip = share * CORES
    contracts = share * n_loc
    chunk = ybuf.shape[3]
    chunks = share // chunk
    parts = up_send.shape[1]
    part = share // parts

    me = lax.axis_index("loc")
    ev = lax.axis_index("ev")
    z, core = me // CORES, me % CORES
    other = 1 - core
    sibling = z * CORES + other

    small = [
        pltpu.make_async_copy(source, target, small_sem.at[i])
        for i, (source, target) in enumerate(
            (
                (curves_hbm, curves_ref),
                (class_hbm, class_ref),
                (expo_hbm, expo_ref),
                (contract_hbm, contract_ref),
                (mask_hbm, mask_ref),
                (year_hbm, year_ref),
                (oret_hbm, oret_ref),
                (olim_hbm, olim_ref),
                (aret_hbm, aret_ref),
                (alim_hbm, alim_ref),
            )
        )
    ]
    loads = wide_sem.shape[1]
    load_cols = locs // loads
    wides = [
        [
            pltpu.make_async_copy(
                source.at[:, pl.ds(i * load_cols, load_cols)],
                target.at[:, pl.ds(i * load_cols, load_cols)],
                wide_sem.at[j, i],
            )
            for j, (source, target) in enumerate(((bins_hbm, bins_ref), (frac_hbm, frac_ref)))
        ]
        for i in range(loads)
    ]
    for copy in small[:5] + [copy for pair in wides for copy in pair] + small[5:]:
        copy.start()

    barrier = pltpu.get_barrier_semaphore()
    for k in range(1, n_loc):
        pl.semaphore_signal(
            barrier, inc=1, device_id={"loc": lax.rem(me + k, n_loc)}, device_id_type=MESH
        )
    for k in range(1, n_ev):
        pl.semaphore_signal(
            barrier, inc=1, device_id={"ev": lax.rem(ev + k, n_ev)}, device_id_type=MESH
        )

    for copy in small[:5]:
        copy.wait()
    curves = curves_ref[...]
    steps = jnp.concatenate([curves[1:] - curves[:-1], jnp.zeros((1, curve_count), F32)], axis=0)
    c_high, c_low = split(jnp.concatenate([curves, steps], axis=0).T)
    blank = jnp.zeros((curve_count, LANES), BF16)
    first_row = (iota((16, LANES), 0) == 0).astype(F32).astype(BF16)
    table_rhs = jnp.concatenate(
        [
            jnp.concatenate([c_high, c_high, c_low, jnp.zeros((16, LANES), BF16)], axis=0),
            jnp.concatenate([blank, blank, blank, first_row], axis=0),
        ],
        axis=1,
    )
    keep = mask_ref[...].astype(F32)
    rows_in_chip = []
    for b in range(blocks):
        cols = pl.ds(b * wide, wide)
        if b * wide % load_cols == 0:
            for copy in wides[b * wide // load_cols]:
                copy.wait()
        contract = contract_ref[b : b + 1, :]
        where_chip = jnp.zeros_like(contract)
        for t in range(1, nz):
            where_chip += (contract >= t * chip).astype(I32)
        rows_in_chip.append(contract - where_chip * chip)
        weight = jnp.where(
            iota((curve_count, wide), 0) == class_ref[b : b + 1, :], expo_ref[b : b + 1, :], 0.0
        )
        w_high, w_low = split(weight)
        chip_rows = jnp.where(iota((16, wide), 0) == 0, where_chip.astype(F32), 0.0).astype(BF16)
        lhs = jnp.concatenate([w_high, w_low, w_high, chip_rows], axis=0)
        both = lax.dot_general(lhs, table_rhs, TN, preferred_element_type=F32)
        table, home = both[:, :LANES], both[:, LANES:]
        place = (bins_ref[:, cols].astype(F32) + frac_ref[:, cols].astype(F32)).T
        knot = place.astype(I32)
        rest = place - knot.astype(F32)
        low = jnp.take_along_axis(table, knot, axis=1, mode="promise_in_bounds")
        rise = jnp.take_along_axis(table, knot + knots, axis=1, mode="promise_in_bounds")
        loss = (low + rest * rise) * keep[b : b + 1, :]
        for t in range(nz):
            spread[cols, pl.ds(t * events, events)] = jnp.where(home == t, loss, 0.0).astype(BF16)

    def partial(which):
        member = jnp.concatenate(
            [
                (iota((share, wide), 0) + which * share == rows).astype(F32).astype(BF16)
                for rows in rows_in_chip
            ],
            axis=1,
        )
        return jnp.dot(member, spread[...], preferred_element_type=F32)

    sums = partial(other)
    for t in range(nz):
        psib[t] = sums[:, t * events : (t + 1) * events]

    sums = partial(core)
    for t in range(nz):
        own[t] = sums[:, t * events : (t + 1) * events]

    for copy in small[5:]:
        copy.wait()
    first = me * share

    def row_of(ref, c):
        start = first + c * chunk
        row = ref[pl.ds(start // LANES, 1), :]
        if share % LANES:
            row = pltpu.roll(
                jnp.broadcast_to(row, (8, LANES)), (LANES - start % LANES) % LANES, 1
            )[:1]
        return row[:, :chunk]

    def column_of(ref, c):
        row = jnp.broadcast_to(row_of(ref, c), (chunk, chunk))
        return jnp.sum(
            jnp.where(iota((chunk, chunk), 0) == iota((chunk, chunk), 1), row, 0.0),
            axis=1,
            keepdims=True,
        )

    orets = [column_of(oret_ref, c) for c in range(chunks)]
    olims = [column_of(olim_ref, c) for c in range(chunks)]
    year_rows = (iota((n_ev * YR_DEV, events), 0) == year_ref[...]).astype(F32).astype(BF16)
    year_rows = jnp.concatenate([year_rows, year_rows], axis=1)

    pl.semaphore_wait(barrier, n_loc - 1 + n_ev - 1)

    def sib_copy(t):
        return pltpu.make_async_remote_copy(
            src_ref=psib.at[t],
            dst_ref=sibr.at[t],
            send_sem=sib_send.at[t],
            recv_sem=sib_recv.at[t],
            device_id={"loc": sibling},
            device_id_type=MESH,
        )

    lower = (z < nz // 2).astype(I32)
    for i in range(nz):
        sib_copy(i + lower * (nz - 1 - 2 * i)).start()

    def hop(t, c, send, recv, into, step):
        rows = pl.ds(c * part, part)
        return pltpu.make_async_remote_copy(
            src_ref=own.at[t, rows],
            dst_ref=into.at[t, rows],
            send_sem=send.at[t, c],
            recv_sem=recv.at[t, c],
            device_id={"loc": me + step},
            device_id_type=MESH,
        )

    up = functools.partial(hop, send=up_send, recv=up_recv, into=upr, step=CORES)
    down = functools.partial(hop, send=dn_send, recv=dn_recv, into=dnr, step=-CORES)

    def pass_on(t, c, way, into, inner):
        rows = pl.ds(c * part, part)
        if c == 0:
            sib_copy(t).wait_recv()

        @pl.when(inner)
        def _():
            way(t, c).wait_recv()
            own[t, rows] = own[t, rows] + sibr[t, rows] + into[t, rows]

        @pl.when(jnp.logical_not(inner))
        def _():
            own[t, rows] = own[t, rows] + sibr[t, rows]

        way(t, c).start()

    for tau in range(nz - 1):
        for c in range(parts):

            @pl.when(z <= tau)
            def _():
                pass_on(nz - 1 - tau + z, c, up, upr, z > 0)

            @pl.when(nz - 1 - z <= tau)
            def _():
                pass_on(tau - (nz - 1) + z, c, down, dnr, z < nz - 1)

    def year_copy(c, k):
        return pltpu.make_async_remote_copy(
            src_ref=ybuf.at[c, lax.rem(ev + k, n_ev)],
            dst_ref=yrecv.at[c, k - 1],
            send_sem=y_send.at[c, k - 1],
            recv_sem=y_recv.at[c, k - 1],
            device_id={"ev": lax.rem(ev + k, n_ev)},
            device_id_type=MESH,
        )

    sib_copy(z).wait_recv()
    for c in range(chunks):
        rows = pl.ds(c * chunk, chunk)
        own[z, rows] = own[z, rows] + sibr[z, rows]
        arrived = range(c * parts // chunks, (c + 1) * parts // chunks)

        @pl.when(z > 0)
        def _():
            for p in arrived:
                up(z, p).wait_recv()
            own[z, rows] = own[z, rows] + upr[z, rows]

        @pl.when(z < nz - 1)
        def _():
            for p in arrived:
                down(z, p).wait_recv()
            own[z, rows] = own[z, rows] + dnr[z, rows]

        occurrence = jnp.minimum(jnp.maximum(own[z, rows] - orets[c], 0.0), olims[c])
        years = lax.dot_general(
            year_rows,
            jnp.concatenate(split(occurrence), axis=1),
            NT,
            preferred_element_type=F32,
        )
        for j in range(n_ev):
            ybuf[c, j] = years[j * YR_DEV : (j + 1) * YR_DEV]
        for k in range(1, n_ev):
            year_copy(c, k).start()

    total = jnp.zeros((1, YR_DEV), F32)
    for c in range(chunks):
        yearly = ybuf[c, ev]
        for k in range(1, n_ev):
            year_copy(c, k).wait_recv()
            yearly += yrecv[c, k - 1]
        annual = jnp.minimum(
            jnp.maximum(yearly - row_of(aret_ref, c), 0.0), row_of(alim_ref, c)
        )
        annual_ref[:, c * chunk : (c + 1) * chunk] = annual
        total += jnp.sum(annual.T, axis=0, keepdims=True)

    msend[:, :YR_DEV] = jnp.broadcast_to(total, (8, YR_DEV))
    msend[:, YR_DEV:] = jnp.zeros((8, LANES - YR_DEV), F32)

    def mean_copy(k):
        return pltpu.make_async_remote_copy(
            src_ref=msend,
            dst_ref=mrecv.at[k - 1],
            send_sem=m_send.at[k - 1],
            recv_sem=m_recv.at[k - 1],
            device_id={"loc": lax.rem(me + k, n_loc)},
            device_id_type=MESH,
        )

    for k in range(1, n_loc):
        mean_copy(k).start()

    for t in range(nz):
        sib_copy(t).wait_send()
    for tau in range(nz - 1):
        for c in range(parts):

            @pl.when(z <= tau)
            def _():
                up(nz - 1 - tau + z, c).wait_send()

            @pl.when(nz - 1 - z <= tau)
            def _():
                down(tau - (nz - 1) + z, c).wait_send()

    for c in range(chunks):
        for k in range(1, n_ev):
            year_copy(c, k).wait_send()

    mean = msend[...]
    for k in range(1, n_loc):
        mean_copy(k).wait_recv()
        mean += mrecv[k - 1]
    mean_ref[...] = (mean / contracts)[:1, :YR_DEV]
    for k in range(1, n_loc):
        mean_copy(k).wait_send()


def solution(mesh):
    n_loc, n_ev = mesh.shape["loc"], mesh.shape["ev"]
    nz = n_loc // CORES

    def local(bins, frac, mask, contract, which, expo, curves, year, oret, olim, aret, alim):
        events, locs = bins.shape
        share = oret.shape[0] // n_loc
        chunk = min(share, LANES)
        chunks = share // chunk
        dma = pltpu.SemaphoreType.DMA
        pieces = pltpu.VMEM((nz, share, events), F32)
        lanes = lambda x: x.reshape(-1, LANES)
        arguments = (
            bins,
            frac,
            mask.T,
            lanes(contract),
            lanes(which),
            lanes(expo),
            curves.T,
            lanes(year),
            lanes(oret),
            lanes(olim),
            lanes(aret),
            lanes(alim),
        )
        annual, mean = pl.pallas_call(
            functools.partial(kernel, n_loc, n_ev),
            out_shape=(
                jax.ShapeDtypeStruct((YR_DEV, share), F32),
                jax.ShapeDtypeStruct((1, YR_DEV), F32),
            ),
            in_specs=[pl.BlockSpec(memory_space=pltpu.HBM)] * 12,
            out_specs=(pl.BlockSpec(memory_space=pltpu.VMEM),) * 2,
            scratch_shapes=[pltpu.VMEM(x.shape, x.dtype) for x in arguments]
            + [
                dma((2, math.gcd(mask.shape[1], 4))),
                dma((10,)),
                pltpu.VMEM((locs, nz * events), BF16),
                pieces,
                pieces,
                pieces,
                pieces,
                pieces,
                pltpu.VMEM((chunks, n_ev, YR_DEV, chunk), F32),
                pltpu.VMEM((chunks, n_ev - 1, YR_DEV, chunk), F32),
                pltpu.VMEM((8, LANES), F32),
                pltpu.VMEM((n_loc - 1, 8, LANES), F32),
                dma((nz,)),
                dma((nz,)),
                dma((nz, 2 * chunks)),
                dma((nz, 2 * chunks)),
                dma((nz, 2 * chunks)),
                dma((nz, 2 * chunks)),
                dma((chunks, n_ev - 1)),
                dma((chunks, n_ev - 1)),
                dma((n_loc - 1,)),
                dma((n_loc - 1,)),
            ],
            compiler_params=pltpu.CompilerParams(
                collective_id=0, has_side_effects=True, vmem_limit_bytes=60 * 2**20
            ),
        )(*arguments)
        return jnp.maximum(annual.T, 0.0), mean.reshape(YR_DEV)

    part = ("grp", "loc")
    in_specs = (
        P("ev", part),
        P("ev", part),
        P("ev", part),
        P(part),
        P(part),
        P(part),
        P(),
        P("ev"),
        P("grp"),
        P("grp"),
        P("grp"),
        P("grp"),
    )
    out_specs = (P(part, "ev"), P(("grp", "ev")))
    return jax.shard_map(local, mesh=mesh, in_specs=in_specs, out_specs=out_specs, check_vma=False)
```
